32 devices in a mesh: row: 4 (over y, x), col: 8 (over z, core).
Axes of the slice: x: 2, y: 2, z: 4, core: 2. Of those that a mesh axis runs over, the one named last changes fastest.
Arguments:
- head_start: float32 [1536, 8192], P('row', 'col'), may hold values from -6 to 6
- recharge: float32 [1536, 8192], P('row', 'col'), may hold values from -4 to 4
- storage: float32 [1536, 8192], P('row', 'col'), may hold values from 0.02 to 0.5
- seg_block: int32 [32768], P(('row', 'col')), may hold values from 0 to 3071
- seg_mask: int32 [32768, 128], P(('row', 'col')), may hold values 0 or 1
- seg_cond: float32 [32768, 128], P(('row', 'col')), may hold values from 0.02 to 0.2
- seg_reach: int32 [32768], P(('row', 'col')), may hold values from 0 to 8191, as said below
- reach_bed: float32 [8192], P(('row', 'col')), may hold values from -1 to 1
- section_start: float32 [8192], P(('row', 'col')), may hold values from 0 to 2
- reach_net: int32 [8192], P(('row', 'col')), may hold values from 0 to 63
- net_inflow: float32 [64], replicated, may hold values from 2 to 16
Outputs:
- head: float32 [1536, 8192], P('row', 'col')
- section: float32 [8192], P(('row', 'col'))
The draws below stay inside these ranges and needn't reach their ends.
Inputs may be any that keep to these rules, and one draw needn't show every extreme that they name: `seg_reach`: A segment on device (i, j) names a reach owned by device (i, j - 1), (i, j) or (i, j + 1), columns taken modulo 8, where reach r is owned by device r // 256 in the numbering i * 8 + j.
All inputs are finite; a program needn't handle non-finite values. No bound on the sum of `seg_mask` on one device may be relied on, other than what follows from the above.
Results may differ from the reference program's by a relative error of at most 0.00029.
Values sent between devices are 32-bit elements; how exact they have to be, the bound alone decides.
A program may use at most 64 MiB of HBM per device.

```python
import math
import jax
import jax.numpy as jnp
from jax import lax

CR = 384
CC = 1024
SEG_DEV = 1024
REACH_DEV = 256
NETS = 64
PICARD = 2
SWEEPS = 4
NR = 1536
NC = 8192
BLK = 3072
SEGS = 32768
R = 8192
N_ROW = 4
N_COL = 8


def draw_seg_reach(key, part):
    first, second = jax.random.split(jax.random.fold_in(key, 11))
    slots = jnp.arange(SEGS, dtype=jnp.int32)
    device = slots // SEG_DEV
    row_pos = device // N_COL
    col_pos = device % N_COL
    offset = jax.random.randint(first, slots.shape, -1, 2, dtype=jnp.int32)
    owner_col = (col_pos + offset + N_COL) % N_COL
    inner = jax.random.randint(second, slots.shape, 0, REACH_DEV, dtype=jnp.int32)
    return ((row_pos * N_COL + owner_col) * REACH_DEV + inner).astype(jnp.int32)


def touch_ends(entries, rng, low, high):
    shape = entries.shape
    place = [jax.random.randint(jax.random.fold_in(rng, axis), (), 0, shape[axis]) for axis in range(len(shape))]
    entries = entries.at[tuple(place)].set(low)
    longest = shape.index(max(shape))
    place[longest] = (place[longest] + 1) % shape[longest]
    return entries.at[tuple(place)].set(high)


def shard_levels(key, shape, shards, smallest, high):
    factor_of = 1.0
    for axis_at, parts in shards:
        heights = jax.random.uniform(jax.random.fold_in(jax.random.fold_in(key, 6), axis_at), (parts,), jnp.float32, smallest / len(shards), high / len(shards))
        factor_of = factor_of * jnp.repeat(jnp.exp(heights), shape[axis_at] // parts).reshape((-1,) + (1,) * (len(shape) - 1 - axis_at))
    return factor_of


def centred(rng, extent, width, bound, pieces=(), held_as=jnp.bfloat16):
    loudness = shard_levels(rng, extent, pieces, -0.22, 0.18) if pieces else 1.0
    result = jax.random.normal(rng, extent, jnp.float32) * width * loudness
    return jnp.minimum(jnp.maximum(result, -bound), bound).astype(held_as)


def setup_inputs(seed: int = 0) -> dict:
    seeds = jax.random.split(jax.random.key(seed), 12)
    return {
        "head_start": centred(seeds[0], (NR, NC), 1.0, 6.0, ((0, 4), (1, 8)), jnp.float32),
        "recharge": centred(seeds[1], (NR, NC), 0.5, 4.0, ((0, 4), (1, 8)), jnp.float32),
        "storage": jnp.clip(jnp.exp(math.log(0.5) - 3.218876 * jax.random.uniform(seeds[2], (NR, NC), jnp.float32) ** shard_levels(seeds[2], (NR, NC), ((0, 4), (1, 8)), -0.2, 0.2)), 0.02, 0.5),
        "seg_block": touch_ends(jax.random.randint(seeds[3], (SEGS,), 0, BLK), jax.random.fold_in(seeds[3], 1), 0, BLK - 1).astype(jnp.int32),
        "seg_mask": touch_ends((jax.random.randint(seeds[4], (SEGS, 128), 0, 4) < 1).astype(jnp.int32), jax.random.fold_in(seeds[4], 1), 0, 1),
        "seg_cond": jnp.clip(jnp.exp(math.log(0.2) - 2.3025851 * jax.random.uniform(seeds[5], (SEGS, 128), jnp.float32) ** shard_levels(seeds[5], (SEGS, 128), ((0, 32),), -0.2, 0.2)), 0.02, 0.2),
        "seg_reach": draw_seg_reach(jax.random.fold_in(seeds[11], 71), 0),
        "reach_bed": jnp.clip(jax.random.uniform(seeds[7], (R,), jnp.float32, -1.0, 1.0) * shard_levels(seeds[7], (R,), ((0, 32),), -0.4, 0.0), -1.0, 1.0),
        "section_start": jnp.clip(2.0 * jax.random.uniform(seeds[8], (R,), jnp.float32) ** shard_levels(seeds[8], (R,), ((0, 32),), -0.2, 0.2), 0.0, 2.0),
        "reach_net": touch_ends(jax.random.randint(seeds[9], (R,), 0, NETS), jax.random.fold_in(seeds[9], 1), 0, NETS - 1).astype(jnp.int32),
        "net_inflow": jnp.clip(jnp.exp(jax.random.uniform(seeds[10], (NETS,), jnp.float32, math.log(2.0), math.log(16.0))), 2.0, 16.0),
    }


def relax(padded, storage, supply, cond, source):
    beside = padded[:-2, 1:-1] + padded[2:, 1:-1] + padded[1:-1, :-2] + padded[1:-1, 2:]
    return (beside + supply + source) / (4.0 + storage + cond)

def reference(head_start, recharge, storage, seg_block, seg_mask, seg_cond, seg_reach, reach_bed, section_start, reach_net, net_inflow):
    devices = N_ROW * N_COL
    blocks = CR * CC // 128

    def to_blocks(grid):
        return grid.reshape(N_ROW, CR, N_COL, CC).transpose(0, 2, 1, 3).reshape(devices * blocks, 128)

    def from_blocks(table):
        return table.reshape(N_ROW, N_COL, CR, CC).transpose(0, 2, 1, 3).reshape(N_ROW * CR, N_COL * CC)
    row_ids = (jnp.arange(SEGS, dtype=jnp.int32) // SEG_DEV * blocks + seg_block).astype(jnp.int32)
    weight = seg_mask.astype(jnp.float32) * seg_cond
    cond = from_blocks(jax.ops.segment_sum(weight, row_ids, devices * blocks))
    inflow = net_inflow[reach_net]
    supply = storage * head_start + recharge
    head = head_start
    section = section_start
    section_seg = section[seg_reach]
    for step in range(PICARD):
        head_seg = to_blocks(head)[row_ids]
        leak = lax.optimization_barrier(jnp.sum(weight * (section_seg[:, None] - head_seg), axis=1))
        total = jax.ops.segment_sum(leak, seg_reach, R)
        section = reach_bed + jnp.sqrt(1.0 + jax.nn.softplus(inflow - total)) - 1.0
        section_seg = section[seg_reach]
        source = from_blocks(jax.ops.segment_sum(weight * section_seg[:, None], row_ids, devices * blocks))
        for sweep in range(SWEEPS):
            head = relax(jnp.pad(head, 1), storage, supply, cond, source)
    return (head, section)
```

```python
import functools

import jax
import jax.numpy as jnp
from jax import lax
from jax.experimental import pallas as pl
from jax.experimental.pallas import tpu as pltpu
from jax.sharding import PartitionSpec as P

PICARD = 2
SWEEPS = 4
L = 128
E = 8
F32 = jnp.float32
BF16 = jnp.bfloat16

DIRS = ((-1, 0), (1, 0), (0, -1), (0, 1), (-1, -1), (-1, 1), (1, -1), (1, 1))
COUNTS = (3, 1, 1, 1)
SUM_STEPS = (1, -1, 2, -2)


def split(x):
    hi = x.astype(BF16)
    return hi, (x - hi.astype(F32)).astype(BF16)


def kernel(
    n_row,
    n_col,
    nets,
    head_in,
    rech,
    stor,
    blk,
    mask,
    conduct,
    reach,
    bed,
    sec0,
    net,
    inflow,
    out_head,
    out_sec,
    place,
    pick,
    put,
    weight,
    slots,
    secseg,
    heads2,
    vals2,
    ga,
    gb,
    supply,
    rhs,
    inv,
    st_send,
    st_recv,
    su_send,
    su_recv,
    *rest,
):
    halo = [rest[6 * e : 6 * e + 6] for e in range(len(COUNTS))]
    st_s, st_r, su_s, su_r, ha_s, ha_r = rest[6 * len(COUNTS) :]
    rows, cols = head_in.shape
    tiles = cols // L
    shift = tiles.bit_length() - 1
    segs = mask.shape[0]
    chunks = segs // L
    h = bed.shape[0]
    reaches = h * L
    ri = lax.axis_index("row")
    ci = lax.axis_index("col")

    def other(dr, dc):
        return (lax.rem(ri + (dr + n_row), n_row), lax.rem(ci + (dc + n_col), n_col))

    partners = list(DIRS) + [(0, 2), (0, -2)]
    barrier = pltpu.get_barrier_semaphore()
    for dr, dc in partners:
        pl.semaphore_signal(
            barrier, inc=1, device_id=other(dr, dc), device_id_type=pl.DeviceIdType.MESH
        )

    def remote(src, dst, send, recv, to):
        return pltpu.make_async_remote_copy(
            src_ref=src,
            dst_ref=dst,
            send_sem=send,
            recv_sem=recv,
            device_id=to,
            device_id_type=pl.DeviceIdType.MESH,
        )

    started = []

    lane = lax.broadcasted_iota(jnp.int32, (L, L), 1)
    sub = lax.broadcasted_iota(jnp.int32, (L, L), 0)
    sub8 = lax.broadcasted_iota(jnp.int32, (8, L), 0)

    net_own = net[...]
    flow = jnp.zeros(net_own.shape, F32)
    for n in range(nets):
        flow = jnp.where(net_own == n, inflow[n], flow)
    st_send[...] = jnp.zeros_like(st_send)
    st_send[0, 0:h] = bed[...]
    st_send[1, 0:h] = flow
    st_send[2, 0:h] = sec0[...]

    b = blk[...]
    place[...] = ((b & (tiles - 1)) * rows + (b >> shift)).astype(F32)

    pl.semaphore_wait(barrier, len(partners))
    st_copies = []
    for k, step in enumerate((1, -1)):
        c = remote(st_send, st_recv.at[k], st_s.at[k], st_r.at[k], other(0, step))
        c.start()
        st_copies.append(c)
    started += st_copies

    own_base = (ri * n_col + ci) * reaches

    def prep(j, _):
        r = pl.ds(pl.multiple_of(j * L, L), L)
        w = mask[r, :].astype(F32) * conduct[r, :]
        weight[r, :] = w
        hi, lo = split(w)
        vals2[r, 0:L] = hi
        vals2[r, L : 2 * L] = lo
        u = reach[pl.ds(j, 1), :] - own_base + reaches
        u = jnp.where(u < 0, u + n_col * reaches, u)
        u = jnp.where(u >= n_col * reaches, u - n_col * reaches, u)
        slots[r, :] = jnp.broadcast_to(u.astype(F32), (L, L)).T.astype(jnp.int32)
        return 0

    lax.fori_loop(0, chunks, prep, 0)

    def build_put(q, _):
        base = q * L
        r = pl.ds(pl.multiple_of(base, L), L)
        for j in range(chunks):
            p = place[j : j + 1, :].astype(jnp.int32) - base
            put[r, j * L : (j + 1) * L] = jnp.where(sub == p, 1.0, 0.0).astype(BF16)
        return 0

    lax.fori_loop(0, rows * tiles // L, build_put, 0)

    def scattered(t):
        r = pl.ds(pl.multiple_of(t * rows, L), rows)
        both = jnp.dot(put[r, :], vals2[...], preferred_element_type=F32)
        return both[:, 0:L] + both[:, L : 2 * L]

    inner = slice(E, E + rows)

    def start_grid(t, _):
        c = pl.ds(pl.multiple_of(t * L, L), L)
        cond = scattered(t)
        s = stor[:, c]
        hd = head_in[:, c]
        ga[inner, c] = hd
        supply[inner, c] = s * hd + rech[:, c]
        inv[inner, c] = 1.0 / (4.0 + s + cond)
        return 0

    lax.fori_loop(0, tiles, start_grid, 0)

    def send_halo(e, arrays):
        s_row, s_col, s_dia, r_row, r_col, r_dia = halo[e]
        for a, x in enumerate(arrays):
            top = x[E : 2 * E, 0:cols]
            bot = x[rows : rows + E, 0:cols]
            s_row[0, a] = top
            s_row[1, a] = bot
            s_col[0, a] = x[inner, 0:L].T[0:E, :]
            s_col[1, a] = x[inner, cols - L : cols].T[L - E : L, :]
            s_dia[0, a] = top[:, 0:L]
            s_dia[1, a] = top[:, cols - L : cols]
            s_dia[2, a] = bot[:, 0:L]
            s_dia[3, a] = bot[:, cols - L : cols]
        copies = []
        for d, (dr, dc) in enumerate(DIRS):
            if dc == 0:
                src, dst = s_row.at[d], r_row.at[d]
            elif dr == 0:
                src, dst = s_col.at[d - 2], r_col.at[d - 2]
            else:
                src, dst = s_dia.at[d - 4], r_dia.at[d - 4]
            c = remote(src, dst, ha_s.at[e, d], ha_r.at[e, d], other(dr, dc))
            c.start()
            copies.append(c)
        return copies

    above = ri > 0
    below = ri < n_row - 1
    lefts = ci > 0
    rights = ci < n_col - 1

    def keep(flag, x):
        return x * jnp.where(flag, 1.0, 0.0).astype(F32)

    def take_halo(e, arrays):
        _, _, _, r_row, r_col, r_dia = halo[e]
        lane8 = lax.broadcasted_iota(jnp.int32, (E, L), 1)
        for a, x in enumerate(arrays):
            x[E + rows : 2 * E + rows, 0:cols] = keep(below, r_row[0, a])
            x[0:E, 0:cols] = keep(above, r_row[1, a])
            beside = jnp.concatenate(
                [
                    keep(rights, r_col[0, a]),
                    jnp.zeros((L - 2 * E, rows), F32),
                    keep(lefts, r_col[1, a]),
                ],
                axis=0,
            )
            x[inner, cols : cols + L] = beside.T
            low = jnp.where(lane8 < L // 2, keep(rights, r_dia[0, a]), keep(lefts, r_dia[1, a]))
            high = jnp.where(lane8 < L // 2, keep(rights, r_dia[2, a]), keep(lefts, r_dia[3, a]))
            x[E + rows : 2 * E + rows, cols : cols + L] = keep(below, low)
            x[0:E, cols : cols + L] = keep(above, high)

    waiting = send_halo(0, (ga, supply, inv))
    started += waiting

    def build_pick(j, _):
        r = pl.ds(pl.multiple_of(j * L, L), L)
        p = jnp.broadcast_to(place[pl.ds(j, 1), :], (L, L)).T.astype(jnp.int32)
        for q in range(rows * tiles // L):
            pick[r, q * L : (q + 1) * L] = jnp.where(p == lane + q * L, 1.0, 0.0).astype(BF16)
        return 0

    lax.fori_loop(0, chunks, build_pick, 0)

    for c in st_copies:
        c.wait_recv()

    def window(k):
        pad = jnp.zeros((8 - 3 * h, L), F32)
        return jnp.concatenate(
            [st_recv[0, k, 0:h], st_send[k, 0:h], st_recv[1, k, 0:h], pad], axis=0
        )

    bed_w = window(0)
    flow_w = window(1)
    sec_w = window(2)

    def spread(sec, fill):
        def one(j, _):
            r = pl.ds(pl.multiple_of(j * L, L), L)
            slot = slots[r, :]
            got = jnp.zeros((L, L), F32)
            for k in range(3 * h):
                got = jnp.where(slot == lane + k * L, sec[k : k + 1, :], got)
            per = jnp.broadcast_to(jnp.sum(got, axis=1, keepdims=True), (L, L))
            secseg[r, :] = per
            if fill:
                hi, lo = split(weight[r, :] * per)
                vals2[r, 0:L] = hi
                vals2[r, L : 2 * L] = lo
            return 0

        lax.fori_loop(0, chunks, one, 0)

    spread(sec_w, False)

    wide = 2 * L if segs % (2 * L) == 0 else L
    groups = (2 * E + rows) // 8

    def sweep(src, dst, last):
        def one(i, carry):
            prev, cur = carry
            r = pl.ds(pl.multiple_of(i * 8, 8), 8)
            nxt = src[pl.ds(pl.multiple_of(jnp.minimum(i + 1, groups - 1) * 8, 8), 8), :]
            s = lax.broadcasted_iota(jnp.int32, cur.shape, 0)
            up = pltpu.roll(jnp.where(s == 7, prev, cur), 1, 0)
            down = pltpu.roll(jnp.where(s == 0, nxt, cur), 7, 0)
            left = pltpu.roll(cur, 1, 1)
            right = pltpu.roll(cur, cols + L - 1, 1)
            new = (((up + down) + (left + right)) + rhs[r, :]) * inv[r, :]
            if last:
                out_head[pl.ds(pl.multiple_of(i * 8 - E, 8), 8), :] = new[:, 0:cols]
            else:
                dst[r, :] = new
            return cur, nxt

        if last:
            lax.fori_loop(1, groups - 1, one, (src[0:8, :], src[8:16, :]))
        else:
            lax.fori_loop(0, groups, one, (src[0:8, :], src[0:8, :]))

    for step in range(PICARD):

        def fill_heads(t, _):
            c = pl.ds(pl.multiple_of(t * L, L), L)
            r = pl.ds(pl.multiple_of(t * rows, L), rows)
            hi, lo = split(ga[inner, c])
            heads2[r, 0:L] = hi
            heads2[r, L : 2 * L] = lo
            return 0

        lax.fori_loop(0, tiles, fill_heads, 0)

        def leaks(j, sums):
            r = pl.ds(pl.multiple_of(j * wide, L), wide)
            both = jnp.dot(pick[r, :], heads2[...], preferred_element_type=F32)
            got = both[:, 0:L] + both[:, L : 2 * L]
            leak = jnp.sum(weight[r, :] * (secseg[r, :] - got), axis=1, keepdims=True)
            slot = slots[r, :]
            lanes = lax.broadcasted_iota(jnp.int32, (wide, L), 1)
            return tuple(
                old + jnp.sum(
                    jnp.where(slot == lanes + k * L, leak, 0.0).reshape(wide // 8, 8, L), axis=0
                )
                for k, old in enumerate(sums)
            )

        sums = lax.fori_loop(
            0, segs // wide, leaks, tuple(jnp.zeros((8, L), F32) for _ in range(3 * h))
        )
        own = jnp.concatenate(
            [jnp.sum(x, axis=0, keepdims=True) for x in sums] + [jnp.zeros((8 - 3 * h, L), F32)],
            axis=0,
        )
        su_send[step] = own
        su_copies = []
        for k, by in enumerate(SUM_STEPS):
            c = remote(
                su_send.at[step],
                su_recv.at[step, k],
                su_s.at[step, k],
                su_r.at[step, k],
                other(0, by),
            )
            c.start()
            su_copies.append(c)
        started += su_copies
        for c in su_copies:
            c.wait_recv()
        zero = jnp.zeros((h, L), F32)
        pad = jnp.zeros((8 - 3 * h, L), F32)
        from_l, from_r, from_ll, from_rr = (su_recv.at[step, k] for k in range(4))
        total = own + jnp.concatenate(
            [
                from_l[h : 2 * h] + from_ll[2 * h : 3 * h],
                from_l[2 * h : 3 * h] + from_r[0:h],
                from_r[h : 2 * h] + from_rr[0:h],
                pad,
            ],
            axis=0,
        )
        x = flow_w - total
        soft = jnp.maximum(x, 0.0) + jnp.log1p(jnp.exp(-jnp.abs(x)))
        sec_w = bed_w + jnp.sqrt(1.0 + soft) - 1.0
        spread(sec_w, True)

        def sources(t, _):
            c = pl.ds(pl.multiple_of(t * L, L), L)
            rhs[inner, c] = supply[inner, c] + scattered(t)
            return 0

        lax.fori_loop(0, tiles, sources, 0)
        mine = send_halo(1 + 2 * step, (rhs,))
        started += mine
        for c in waiting:
            c.wait_recv()
        if step == 0:
            take_halo(0, (ga, supply, inv))
        else:
            take_halo(2, (ga,))
        for c in mine:
            c.wait_recv()
        take_halo(1 + 2 * step, (rhs,))
        bufs = (ga, gb)
        for k in range(SWEEPS):
            last = step == PICARD - 1 and k == SWEEPS - 1
            sweep(bufs[k % 2], bufs[(k + 1) % 2], last)
        if step < PICARD - 1:
            waiting = send_halo(2, (ga,))
            started += waiting

    out_sec[...] = sec_w[h : 2 * h, :]
    for c in started:
        c.wait_send()


def body(n_row, n_col, head, rech, stor, blk, mask, cond, reach, bed, sec, net, inflow):
    rows, cols = head.shape
    segs = blk.shape[0]
    reaches = bed.shape[0]
    blocks = rows * cols // L
    h = reaches // L
    vmem = pl.BlockSpec(memory_space=pltpu.VMEM)
    grid = pltpu.VMEM((rows + 2 * E, cols + L), F32)
    scratch = [
        pltpu.VMEM((segs // L, L), F32),
        pltpu.VMEM((segs, blocks), BF16),
        pltpu.VMEM((blocks, segs), BF16),
        pltpu.VMEM((segs, L), F32),
        pltpu.VMEM((segs, L), jnp.int32),
        pltpu.VMEM((segs, L), F32),
        pltpu.VMEM((blocks, 2 * L), BF16),
        pltpu.VMEM((segs, 2 * L), BF16),
        grid,
        grid,
        grid,
        grid,
        grid,
        pltpu.VMEM((3, 8, L), F32),
        pltpu.VMEM((2, 3, 8, L), F32),
        pltpu.VMEM((PICARD, 8, L), F32),
        pltpu.VMEM((PICARD, 4, 8, L), F32),
    ]
    for n in COUNTS:
        for _ in range(2):
            scratch += [
                pltpu.VMEM((2, n, E, cols), F32),
                pltpu.VMEM((2, n, E, rows), F32),
                pltpu.VMEM((4, n, E, L), F32),
            ]
    dma = pltpu.SemaphoreType.DMA
    scratch += [
        dma((2,)),
        dma((2,)),
        dma((PICARD, 4)),
        dma((PICARD, 4)),
        dma((len(COUNTS), 8)),
        dma((len(COUNTS), 8)),
    ]
    out_head, out_sec = pl.pallas_call(
        functools.partial(kernel, n_row, n_col, inflow.shape[0]),
        out_shape=(
            jax.ShapeDtypeStruct((rows, cols), F32),
            jax.ShapeDtypeStruct((h, L), F32),
        ),
        in_specs=[vmem] * 10 + [pl.BlockSpec(memory_space=pltpu.SMEM)],
        out_specs=(vmem, vmem),
        scratch_shapes=scratch,
        compiler_params=pltpu.CompilerParams(
            collective_id=0, has_side_effects=True, vmem_limit_bytes=56 * 1024 * 1024
        ),
    )(
        head,
        rech,
        stor,
        blk.reshape(segs // L, L),
        mask,
        cond,
        reach.reshape(segs // L, L),
        bed.reshape(h, L),
        sec.reshape(h, L),
        net.reshape(h, L),
        inflow,
    )
    return out_head, out_sec.reshape(reaches)


def solution(mesh):
    placed = (
        P("row", "col"),
        P("row", "col"),
        P("row", "col"),
        P(("row", "col")),
        P(("row", "col"), None),
        P(("row", "col"), None),
        P(("row", "col")),
        P(("row", "col")),
        P(("row", "col")),
        P(("row", "col")),
        P(),
    )
    return jax.shard_map(
        functools.partial(body, mesh.shape["row"], mesh.shape["col"]),
        mesh=mesh,
        in_specs=placed,
        out_specs=(P("row", "col"), P(("row", "col"))),
        check_vma=False,
    )
```

```python
import functools

import jax
import jax.numpy as jnp
from jax import lax
from jax.experimental import pallas as pl
from jax.experimental.pallas import tpu as pltpu
from jax.sharding import PartitionSpec as P

PICARD = 2
SWEEPS = 4
L = 128
E = 8
F32 = jnp.float32
BF16 = jnp.bfloat16

DIRS = ((-1, 0), (1, 0), (0, -1), (0, 1), (-1, -1), (-1, 1), (1, -1), (1, 1))
COUNTS = (2, 1, 1, 1)
SUM_STEPS = (1, -1, 2, -2)


def split(x):
    hi = x.astype(BF16)
    return hi, (x - hi.astype(F32)).astype(BF16)


def kernel(
    n_row,
    n_col,
    nets,
    head_in,
    rech,
    stor,
    blk,
    mask,
    conduct,
    reach,
    bed,
    sec0,
    net,
    inflow,
    out_head,
    out_sec,
    place,
    pick,
    put,
    weight,
    slots,
    secseg,
    heads2,
    vals2,
    ga,
    gb,
    supply,
    rhs,
    inv,
    st_send,
    st_recv,
    su_send,
    su_recv,
    *rest,
):
    halo = [rest[6 * e : 6 * e + 6] for e in range(len(COUNTS))]
    st_s, st_r, su_s, su_r, ha_s, ha_r, lo_s = rest[6 * len(COUNTS) :]
    rows, cols = head_in.shape
    tiles = cols // L
    shift = tiles.bit_length() - 1
    segs = mask.shape[0]
    chunks = segs // L
    h = bed.shape[0]
    reaches = h * L
    ri = lax.axis_index("row")
    ci = lax.axis_index("col")

    def other(dr, dc):
        return (lax.rem(ri + (dr + n_row), n_row), lax.rem(ci + (dc + n_col), n_col))

    partners = list(DIRS) + [(0, 2), (0, -2)]
    barrier = pltpu.get_barrier_semaphore()
    for dr, dc in partners:
        pl.semaphore_signal(
            barrier, inc=1, device_id=other(dr, dc), device_id_type=pl.DeviceIdType.MESH
        )

    def remote(src, dst, send, recv, to):
        return pltpu.make_async_remote_copy(
            src_ref=src,
            dst_ref=dst,
            send_sem=send,
            recv_sem=recv,
            device_id=to,
            device_id_type=pl.DeviceIdType.MESH,
        )

    started = []
    inner = slice(E, E + rows)
    locals_ = [
        pltpu.make_async_copy(x, y.at[inner, 0:cols], lo_s.at[k])
        for k, (x, y) in enumerate(((head_in, ga), (stor, inv), (rech, supply)))
    ]
    for c in locals_:
        c.start()

    lane = lax.broadcasted_iota(jnp.int32, (L, L), 1)
    sub = lax.broadcasted_iota(jnp.int32, (L, L), 0)
    sub8 = lax.broadcasted_iota(jnp.int32, (8, L), 0)

    net_own = net[...]
    flow = jnp.zeros(net_own.shape, F32)
    for n in range(nets):
        flow = jnp.where(net_own == n, inflow[n], flow)
    st_send[...] = jnp.zeros_like(st_send)
    st_send[0, 0:h] = bed[...]
    st_send[1, 0:h] = flow
    st_send[2, 0:h] = sec0[...]

    b = blk[...]
    place[...] = ((b & (tiles - 1)) * rows + (b >> shift)).astype(F32)

    pl.semaphore_wait(barrier, len(partners))
    st_copies = []
    for k, step in enumerate((1, -1)):
        c = remote(st_send, st_recv.at[k], st_s.at[k], st_r.at[k], other(0, step))
        c.start()
        st_copies.append(c)
    started += st_copies

    own_base = (ri * n_col + ci) * reaches

    def prep(j, _):
        r = pl.ds(pl.multiple_of(j * L, L), L)
        w = mask[r, :].astype(F32) * conduct[r, :]
        weight[r, :] = w
        hi, lo = split(w)
        vals2[r, 0:L] = hi
        vals2[r, L : 2 * L] = lo
        u = reach[pl.ds(j, 1), :] - own_base + reaches
        u = jnp.where(u < 0, u + n_col * reaches, u)
        u = jnp.where(u >= n_col * reaches, u - n_col * reaches, u)
        slots[r, :] = jnp.broadcast_to(u.astype(F32), (L, L)).T.astype(jnp.int32)
        return 0

    lax.fori_loop(0, chunks, prep, 0)

    def build_put(q, _):
        base = q * L
        r = pl.ds(pl.multiple_of(base, L), L)
        for j in range(chunks):
            p = place[j : j + 1, :].astype(jnp.int32) - base
            put[r, j * L : (j + 1) * L] = jnp.where(sub == p, 1.0, 0.0).astype(BF16)
        return 0


    def scattered(t):
        r = pl.ds(pl.multiple_of(t * rows, L), rows)
        both = jnp.dot(put[r, :], vals2[...], preferred_element_type=F32)
        return both[:, 0:L] + both[:, L : 2 * L]

    def start_grid(t, _):
        c = pl.ds(pl.multiple_of(t * L, L), L)
        cond = scattered(t)
        s = inv[inner, c]
        supply[inner, c] = s * ga[inner, c] + supply[inner, c]
        inv[inner, c] = 1.0 / (4.0 + s + cond)
        return 0

    def send_halo(e, arrays):
        s_row, s_col, s_dia, r_row, r_col, r_dia = halo[e]
        for a, x in enumerate(arrays):
            top = x[E : 2 * E, 0:cols]
            bot = x[rows : rows + E, 0:cols]
            s_row[0, a] = top
            s_row[1, a] = bot
            s_col[0, a] = x[inner, 0:L].T[0:E, :]
            s_col[1, a] = x[inner, cols - L : cols].T[L - E : L, :]
            s_dia[0, a] = top[:, 0:L]
            s_dia[1, a] = top[:, cols - L : cols]
            s_dia[2, a] = bot[:, 0:L]
            s_dia[3, a] = bot[:, cols - L : cols]
        copies = []
        for d, (dr, dc) in enumerate(DIRS):
            if dc == 0:
                src, dst = s_row.at[d], r_row.at[d]
            elif dr == 0:
                src, dst = s_col.at[d - 2], r_col.at[d - 2]
            else:
                src, dst = s_dia.at[d - 4], r_dia.at[d - 4]
            c = remote(src, dst, ha_s.at[e, d], ha_r.at[e, d], other(dr, dc))
            c.start()
            copies.append(c)
        return copies

    above = ri > 0
    below = ri < n_row - 1
    lefts = ci > 0
    rights = ci < n_col - 1

    def keep(flag, x):
        return x * jnp.where(flag, 1.0, 0.0).astype(F32)

    def take_halo(e, arrays):
        _, _, _, r_row, r_col, r_dia = halo[e]
        lane8 = lax.broadcasted_iota(jnp.int32, (E, L), 1)
        for a, x in enumerate(arrays):
            x[E + rows : 2 * E + rows, 0:cols] = keep(below, r_row[0, a])
            x[0:E, 0:cols] = keep(above, r_row[1, a])
            beside = jnp.concatenate(
                [
                    keep(rights, r_col[0, a]),
                    jnp.zeros((L - 2 * E, rows), F32),
                    keep(lefts, r_col[1, a]),
                ],
                axis=0,
            )
            x[inner, cols : cols + L] = beside.T
            low = jnp.where(lane8 < L // 2, keep(rights, r_dia[0, a]), keep(lefts, r_dia[1, a]))
            high = jnp.where(lane8 < L // 2, keep(rights, r_dia[2, a]), keep(lefts, r_dia[3, a]))
            x[E + rows : 2 * E + rows, cols : cols + L] = keep(below, low)
            x[0:E, cols : cols + L] = keep(above, high)

    def build_pick(j, _):
        r = pl.ds(pl.multiple_of(j * L, L), L)
        p = jnp.broadcast_to(place[pl.ds(j, 1), :], (L, L)).T.astype(jnp.int32)
        for q in range(rows * tiles // L):
            pick[r, q * L : (q + 1) * L] = jnp.where(p == lane + q * L, 1.0, 0.0).astype(BF16)
        return 0

    lax.fori_loop(0, chunks, build_pick, 0)

    def fill_heads(t, _):
        c = pl.ds(pl.multiple_of(t * L, L), L)
        r = pl.ds(pl.multiple_of(t * rows, L), rows)
        hi, lo = split(ga[inner, c])
        heads2[r, 0:L] = hi
        heads2[r, L : 2 * L] = lo
        return 0

    locals_[0].wait()
    lax.fori_loop(0, tiles, fill_heads, 0)

    for c in st_copies:
        c.wait_recv()

    def window(k):
        pad = jnp.zeros((8 - 3 * h, L), F32)
        return jnp.concatenate(
            [st_recv[0, k, 0:h], st_send[k, 0:h], st_recv[1, k, 0:h], pad], axis=0
        )

    bed_w = window(0)
    flow_w = window(1)
    sec_w = window(2)

    def spread(sec, fill):
        def one(j, _):
            r = pl.ds(pl.multiple_of(j * L, L), L)
            slot = slots[r, :]
            got = jnp.zeros((L, L), F32)
            for k in range(3 * h):
                got = jnp.where(slot == lane + k * L, sec[k : k + 1, :], got)
            per = jnp.broadcast_to(jnp.sum(got, axis=1, keepdims=True), (L, L))
            secseg[r, :] = per
            if fill:
                hi, lo = split(weight[r, :] * per)
                vals2[r, 0:L] = hi
                vals2[r, L : 2 * L] = lo
            return 0

        lax.fori_loop(0, chunks, one, 0)

    spread(sec_w, False)

    wide = 4 * L if segs % (4 * L) == 0 else L
    groups = (2 * E + rows) // 8

    def sweep(src, dst, last):
        first = 1 if last else 0
        count = groups - 2 * first
        unit = max(u for u in range(1, 7) if count % u == 0)

        def some(g, carry):
            prev, cur = carry
            for u in range(unit):
                i = first + g * unit + u
                r = pl.ds(pl.multiple_of(i * 8, 8), 8)
                nxt = src[pl.ds(pl.multiple_of(jnp.minimum(i + 1, groups - 1) * 8, 8), 8), :]
                s = lax.broadcasted_iota(jnp.int32, cur.shape, 0)
                up = pltpu.roll(jnp.where(s == 7, prev, cur), 1, 0)
                down = pltpu.roll(jnp.where(s == 0, nxt, cur), 7, 0)
                left = pltpu.roll(cur, 1, 1)
                right = pltpu.roll(cur, cols + L - 1, 1)
                new = (((up + down) + (left + right)) + rhs[r, :]) * inv[r, :]
                if last:
                    out_head[pl.ds(pl.multiple_of(i * 8 - E, 8), 8), :] = new[:, 0:cols]
                else:
                    dst[r, :] = new
                prev, cur = cur, nxt
            return prev, cur

        lax.fori_loop(0, count // unit, some, (src[0:8, :], src[8 * first : 8 * first + 8, :]))

    def clear_halo(x):
        x[0:E, :] = jnp.zeros((E, cols + L), F32)
        x[E + rows : 2 * E + rows, :] = jnp.zeros((E, cols + L), F32)
        x[inner, cols : cols + L] = jnp.zeros((rows, L), F32)

    for step in range(PICARD):

        def leaks(j, sums):
            r = pl.ds(pl.multiple_of(j * wide, L), wide)
            both = jnp.dot(pick[r, :], heads2[...], preferred_element_type=F32)
            got = both[:, 0:L] + both[:, L : 2 * L]
            leak = jnp.sum(weight[r, :] * (secseg[r, :] - got), axis=1, keepdims=True)
            slot = slots[r, :]
            lanes = lax.broadcasted_iota(jnp.int32, (wide, L), 1)
            return tuple(
                old + jnp.sum(
                    jnp.where(slot == lanes + k * L, leak, 0.0).reshape(wide // 8, 8, L), axis=0
                )
                for k, old in enumerate(sums)
            )

        sums = lax.fori_loop(
            0, segs // wide, leaks, tuple(jnp.zeros((8, L), F32) for _ in range(3 * h))
        )
        own = jnp.concatenate(
            [jnp.sum(x, axis=0, keepdims=True) for x in sums] + [jnp.zeros((8 - 3 * h, L), F32)],
            axis=0,
        )
        su_send[step] = own
        su_copies = []
        for k, by in enumerate(SUM_STEPS):
            c = remote(
                su_send.at[step],
                su_recv.at[step, k],
                su_s.at[step, k],
                su_r.at[step, k],
                other(0, by),
            )
            c.start()
            su_copies.append(c)
        started += su_copies
        if step == 0:
            lax.fori_loop(0, rows * tiles // L, build_put, 0)
            locals_[1].wait()
            locals_[2].wait()
            lax.fori_loop(0, tiles, start_grid, 0)
            waiting = send_halo(0, (ga, inv))
            started += waiting
        else:
            for c in waiting:
                c.wait_recv()
            take_halo(2, (ga,))
        clear_halo(rhs)
        for c in su_copies:
            c.wait_recv()
        pad = jnp.zeros((8 - 3 * h, L), F32)
        from_l, from_r, from_ll, from_rr = (su_recv.at[step, k] for k in range(4))
        total = own + jnp.concatenate(
            [
                from_l[h : 2 * h] + from_ll[2 * h : 3 * h],
                from_l[2 * h : 3 * h] + from_r[0:h],
                from_r[h : 2 * h] + from_rr[0:h],
                pad,
            ],
            axis=0,
        )
        x = flow_w - total
        soft = jnp.maximum(x, 0.0) + jnp.log1p(jnp.exp(-jnp.abs(x)))
        sec_w = bed_w + jnp.sqrt(1.0 + soft) - 1.0
        spread(sec_w, True)

        def sources(t, _):
            c = pl.ds(pl.multiple_of(t * L, L), L)
            rhs[inner, c] = supply[inner, c] + scattered(t)
            return 0

        lax.fori_loop(0, tiles, sources, 0)
        mine = send_halo(1 + 2 * step, (rhs,))
        started += mine
        if step == 0:
            for c in waiting:
                c.wait_recv()
            take_halo(0, (ga, inv))
        bufs = (ga, gb)
        for k in range(SWEEPS):
            last = step == PICARD - 1 and k == SWEEPS - 1
            sweep(bufs[k % 2], bufs[(k + 1) % 2], last)
            if k == 0:
                for c in mine:
                    c.wait_recv()
                take_halo(1 + 2 * step, (rhs,))
                for r, c in (
                    (slice(0, E), slice(0, cols + L)),
                    (slice(E + rows, 2 * E + rows), slice(0, cols + L)),
                    (inner, slice(cols, cols + L)),
                ):
                    gb[r, c] = gb[r, c] + rhs[r, c] * inv[r, c]
        if step < PICARD - 1:
            waiting = send_halo(2, (ga,))
            started += waiting
            lax.fori_loop(0, tiles, fill_heads, 0)

    out_sec[...] = sec_w[h : 2 * h, :]
    for c in started:
        c.wait_send()


def body(n_row, n_col, head, rech, stor, blk, mask, cond, reach, bed, sec, net, inflow):
    rows, cols = head.shape
    segs = blk.shape[0]
    reaches = bed.shape[0]
    blocks = rows * cols // L
    h = reaches // L
    vmem = pl.BlockSpec(memory_space=pltpu.VMEM)
    grid = pltpu.VMEM((rows + 2 * E, cols + L), F32)
    scratch = [
        pltpu.VMEM((segs // L, L), F32),
        pltpu.VMEM((segs, blocks), BF16),
        pltpu.VMEM((blocks, segs), BF16),
        pltpu.VMEM((segs, L), F32),
        pltpu.VMEM((segs, L), jnp.int32),
        pltpu.VMEM((segs, L), F32),
        pltpu.VMEM((blocks, 2 * L), BF16),
        pltpu.VMEM((segs, 2 * L), BF16),
        grid,
        grid,
        grid,
        grid,
        grid,
        pltpu.VMEM((3, 8, L), F32),
        pltpu.VMEM((2, 3, 8, L), F32),
        pltpu.VMEM((PICARD, 8, L), F32),
        pltpu.VMEM((PICARD, 4, 8, L), F32),
    ]
    for n in COUNTS:
        for _ in range(2):
            scratch += [
                pltpu.VMEM((2, n, E, cols), F32),
                pltpu.VMEM((2, n, E, rows), F32),
                pltpu.VMEM((4, n, E, L), F32),
            ]
    dma = pltpu.SemaphoreType.DMA
    scratch += [
        dma((2,)),
        dma((2,)),
        dma((PICARD, 4)),
        dma((PICARD, 4)),
        dma((len(COUNTS), 8)),
        dma((len(COUNTS), 8)),
        dma((3,)),
    ]
    out_head, out_sec = pl.pallas_call(
        functools.partial(kernel, n_row, n_col, inflow.shape[0]),
        out_shape=(
            jax.ShapeDtypeStruct((rows, cols), F32),
            jax.ShapeDtypeStruct((h, L), F32),
        ),
        in_specs=[pl.BlockSpec(memory_space=pl.ANY)] * 3 + [vmem] * 7 + [pl.BlockSpec(memory_space=pltpu.SMEM)],
        out_specs=(vmem, vmem),
        scratch_shapes=scratch,
        compiler_params=pltpu.CompilerParams(
            collective_id=0, has_side_effects=True, vmem_limit_bytes=56 * 1024 * 1024
        ),
    )(
        head,
        rech,
        stor,
        blk.reshape(segs // L, L),
        mask,
        cond,
        reach.reshape(segs // L, L),
        bed.reshape(h, L),
        sec.reshape(h, L),
        net.reshape(h, L),
        inflow,
    )
    return out_head, out_sec.reshape(reaches)


def solution(mesh):
    placed = (
        P("row", "col"),
        P("row", "col"),
        P("row", "col"),
        P(("row", "col")),
        P(("row", "col"), None),
        P(("row", "col"), None),
        P(("row", "col")),
        P(("row", "col")),
        P(("row", "col")),
        P(("row", "col")),
        P(),
    )
    return jax.shard_map(
        functools.partial(body, mesh.shape["row"], mesh.shape["col"]),
        mesh=mesh,
        in_specs=placed,
        out_specs=(P("row", "col"), P(("row", "col"))),
        check_vma=False,
    )
```

```python
import functools

import jax
import jax.numpy as jnp
from jax import lax
from jax.experimental import pallas as pl
from jax.experimental.pallas import tpu as pltpu
from jax.sharding import PartitionSpec as P

PICARD = 2
SWEEPS = 4
L = 128
E = 8
F32 = jnp.float32
BF16 = jnp.bfloat16

DIRS = ((-1, 0), (1, 0), (0, -1), (0, 1), (-1, -1), (-1, 1), (1, -1), (1, 1))
COUNTS = (2, 1, 1, 1)
PARTS = 8
SUM_STEPS = (1, -1, 2, -2)


def several(count, most, one):
    unit = max(u for u in range(1, most + 1) if count % u == 0)

    def some(g, _):
        for u in range(unit):
            one(g * unit + u, 0)
        return 0

    lax.fori_loop(0, count // unit, some, 0)


def split(x):
    hi = x.astype(BF16)
    return hi, (x - hi.astype(F32)).astype(BF16)


def kernel(
    n_row,
    n_col,
    nets,
    head_in,
    rech,
    stor,
    blk,
    mask,
    conduct,
    reach,
    bed,
    sec0,
    net,
    inflow,
    out_head,
    out_sec,
    place,
    pick,
    put,
    weight,
    slots,
    secseg,
    heads2,
    vals2,
    ga,
    gb,
    supply,
    rhs,
    inv,
    st_send,
    st_recv,
    su_send,
    su_recv,
    *rest,
):
    halo = [rest[6 * e : 6 * e + 6] for e in range(len(COUNTS))]
    st_s, st_r, su_s, su_r, ha_s, ha_r, lo_s = rest[6 * len(COUNTS) :]
    rows, cols = head_in.shape
    tiles = cols // L
    shift = tiles.bit_length() - 1
    segs = mask.shape[0]
    chunks = segs // L
    h = bed.shape[0]
    reaches = h * L
    ri = lax.axis_index("row")
    ci = lax.axis_index("col")

    def other(dr, dc):
        return (lax.rem(ri + (dr + n_row), n_row), lax.rem(ci + (dc + n_col), n_col))

    partners = list(DIRS) + [(0, 2), (0, -2)]
    barrier = pltpu.get_barrier_semaphore()
    for dr, dc in partners:
        pl.semaphore_signal(
            barrier, inc=1, device_id=other(dr, dc), device_id_type=pl.DeviceIdType.MESH
        )

    def remote(src, dst, send, recv, to):
        return pltpu.make_async_remote_copy(
            src_ref=src,
            dst_ref=dst,
            send_sem=send,
            recv_sem=recv,
            device_id=to,
            device_id_type=pl.DeviceIdType.MESH,
        )

    started = []
    inner = slice(E, E + rows)
    locals_ = [
        pltpu.make_async_copy(x, y.at[inner, 0:cols], lo_s.at[k])
        for k, (x, y) in enumerate(((head_in, ga), (stor, inv), (rech, supply)))
    ]
    for c in locals_:
        c.start()

    lane = lax.broadcasted_iota(jnp.int32, (L, L), 1)
    sub = lax.broadcasted_iota(jnp.int32, (L, L), 0)
    sub8 = lax.broadcasted_iota(jnp.int32, (8, L), 0)

    net_own = net[...]
    flow = jnp.zeros(net_own.shape, F32)
    for n in range(nets):
        flow = jnp.where(net_own == n, inflow[n], flow)
    st_send[...] = jnp.zeros_like(st_send)
    st_send[0, 0:h] = bed[...]
    st_send[1, 0:h] = flow
    st_send[2, 0:h] = sec0[...]

    b = blk[...]
    place[...] = ((b & (tiles - 1)) * rows + (b >> shift)).astype(F32)

    pl.semaphore_wait(barrier, len(partners))
    st_copies = []
    for k, step in enumerate((1, -1)):
        c = remote(st_send, st_recv.at[k], st_s.at[k], st_r.at[k], other(0, step))
        c.start()
        st_copies.append(c)
    started += st_copies

    own_base = (ri * n_col + ci) * reaches

    def prep(j, _):
        r = pl.ds(pl.multiple_of(j * L, L), L)
        w = mask[r, :].astype(F32) * conduct[r, :]
        weight[r, :] = w
        hi, lo = split(w)
        vals2[r, 0:L] = hi
        vals2[r, L : 2 * L] = lo
        u = reach[pl.ds(j, 1), :] - own_base + reaches
        u = jnp.where(u < 0, u + n_col * reaches, u)
        u = jnp.where(u >= n_col * reaches, u - n_col * reaches, u)
        slots[r, :] = jnp.broadcast_to(u.astype(F32), (L, L)).T.astype(jnp.int32)
        return 0

    several(chunks, 4, prep)

    def build_put(q, _):
        base = q * L
        r = pl.ds(pl.multiple_of(base, L), L)
        for j in range(chunks):
            p = place[j : j + 1, :].astype(jnp.int32) - base
            put[r, j * L : (j + 1) * L] = jnp.where(sub == p, 1.0, 0.0).astype(BF16)
        return 0


    def scattered(t):
        r = pl.ds(pl.multiple_of(t * rows, L), rows)
        both = jnp.dot(put[r, :], vals2[...], preferred_element_type=F32)
        return both[:, 0:L] + both[:, L : 2 * L]

    def start_grid(t, _):
        c = pl.ds(pl.multiple_of(t * L, L), L)
        cond = scattered(t)
        s = inv[inner, c]
        supply[inner, c] = s * ga[inner, c] + supply[inner, c]
        inv[inner, c] = 1.0 / (4.0 + s + cond)
        return 0

    def send_halo(e, arrays):
        s_row, s_col, s_dia, r_row, r_col, r_dia = halo[e]
        for a, x in enumerate(arrays):
            top = x[E : 2 * E, 0:cols]
            bot = x[rows : rows + E, 0:cols]
            s_row[0, a] = top
            s_row[1, a] = bot
            s_col[0, a] = x[inner, 0:L].T[0:E, :]
            s_col[1, a] = x[inner, cols - L : cols].T[L - E : L, :]
            s_dia[0, a] = top[:, 0:L]
            s_dia[1, a] = top[:, cols - L : cols]
            s_dia[2, a] = bot[:, 0:L]
            s_dia[3, a] = bot[:, cols - L : cols]
        copies = []
        for d, (dr, dc) in enumerate(DIRS):
            if dc == 0:
                src, dst = s_row.at[d], r_row.at[d]
            elif dr == 0:
                src, dst = s_col.at[d - 2], r_col.at[d - 2]
            else:
                src, dst = s_dia.at[d - 4], r_dia.at[d - 4]
            c = remote(src, dst, ha_s.at[e, d], ha_r.at[e, d], other(dr, dc))
            c.start()
            copies.append(c)
        return copies

    above = ri > 0
    below = ri < n_row - 1
    lefts = ci > 0
    rights = ci < n_col - 1

    def keep(flag, x):
        return x * jnp.where(flag, 1.0, 0.0).astype(F32)

    def take_halo(e, arrays):
        _, _, _, r_row, r_col, r_dia = halo[e]
        lane8 = lax.broadcasted_iota(jnp.int32, (E, L), 1)
        for a, x in enumerate(arrays):
            x[E + rows : 2 * E + rows, 0:cols] = keep(below, r_row[0, a])
            x[0:E, 0:cols] = keep(above, r_row[1, a])
            beside = jnp.concatenate(
                [
                    keep(rights, r_col[0, a]),
                    jnp.zeros((L - 2 * E, rows), F32),
                    keep(lefts, r_col[1, a]),
                ],
                axis=0,
            )
            x[inner, cols : cols + L] = beside.T
            low = jnp.where(lane8 < L // 2, keep(rights, r_dia[0, a]), keep(lefts, r_dia[1, a]))
            high = jnp.where(lane8 < L // 2, keep(rights, r_dia[2, a]), keep(lefts, r_dia[3, a]))
            x[E + rows : 2 * E + rows, cols : cols + L] = keep(below, low)
            x[0:E, cols : cols + L] = keep(above, high)

    def build_pick(j, _):
        r = pl.ds(pl.multiple_of(j * L, L), L)
        p = jnp.broadcast_to(place[pl.ds(j, 1), :], (L, L)).T.astype(jnp.int32)
        for q in range(rows * tiles // L):
            pick[r, q * L : (q + 1) * L] = jnp.where(p == lane + q * L, 1.0, 0.0).astype(BF16)
        return 0

    several(chunks, 2, build_pick)

    def fill_heads(t, _):
        c = pl.ds(pl.multiple_of(t * L, L), L)
        r = pl.ds(pl.multiple_of(t * rows, L), rows)
        hi, lo = split(ga[inner, c])
        heads2[r, 0:L] = hi
        heads2[r, L : 2 * L] = lo
        return 0

    locals_[0].wait()
    several(tiles, 4, fill_heads)

    for c in st_copies:
        c.wait_recv()

    def window(k):
        pad = jnp.zeros((8 - 3 * h, L), F32)
        return jnp.concatenate(
            [st_recv[0, k, 0:h], st_send[k, 0:h], st_recv[1, k, 0:h], pad], axis=0
        )

    bed_w = window(0)
    flow_w = window(1)
    sec_w = window(2)

    def spread(sec, fill):
        def one(j, _):
            r = pl.ds(pl.multiple_of(j * L, L), L)
            slot = slots[r, :]
            got = jnp.zeros((L, L), F32)
            for k in range(3 * h):
                got = jnp.where(slot == lane + k * L, sec[k : k + 1, :], got)
            per = jnp.broadcast_to(jnp.sum(got, axis=1, keepdims=True), (L, L))
            secseg[r, :] = per
            if fill:
                hi, lo = split(weight[r, :] * per)
                vals2[r, 0:L] = hi
                vals2[r, L : 2 * L] = lo
            return 0

        several(chunks, 8, one)

    spread(sec_w, False)

    wide = 4 * L if segs % (4 * L) == 0 else L
    groups = (2 * E + rows) // 8

    def sweep(src, dst, last):
        first = 1 if last else 0
        count = groups - 2 * first
        unit = max(u for u in range(1, 13) if count % u == 0)

        def some(g, carry):
            prev, cur = carry
            for u in range(unit):
                i = first + g * unit + u
                r = pl.ds(pl.multiple_of(i * 8, 8), 8)
                nxt = src[pl.ds(pl.multiple_of(jnp.minimum(i + 1, groups - 1) * 8, 8), 8), :]
                s = lax.broadcasted_iota(jnp.int32, cur.shape, 0)
                up = pltpu.roll(jnp.where(s == 7, prev, cur), 1, 0)
                down = pltpu.roll(jnp.where(s == 0, nxt, cur), 7, 0)
                left = pltpu.roll(cur, 1, 1)
                right = pltpu.roll(cur, cols + L - 1, 1)
                new = (((up + down) + (left + right)) + rhs[r, :]) * inv[r, :]
                if last:
                    out_head[pl.ds(pl.multiple_of(i * 8 - E, 8), 8), :] = new[:, 0:cols]
                else:
                    dst[r, :] = new
                prev, cur = cur, nxt
            return prev, cur

        lax.fori_loop(0, count // unit, some, (src[0:8, :], src[8 * first : 8 * first + 8, :]))

    def clear_halo(x):
        x[0:E, :] = jnp.zeros((E, cols + L), F32)
        x[E + rows : 2 * E + rows, :] = jnp.zeros((E, cols + L), F32)
        x[inner, cols : cols + L] = jnp.zeros((rows, L), F32)

    for step in range(PICARD):

        def leaks(j, sums):
            r = pl.ds(pl.multiple_of(j * wide, L), wide)
            both = jnp.dot(pick[r, :], heads2[...], preferred_element_type=F32)
            got = both[:, 0:L] + both[:, L : 2 * L]
            leak = jnp.sum(weight[r, :] * (secseg[r, :] - got), axis=1, keepdims=True)
            slot = slots[r, :]
            lanes = lax.broadcasted_iota(jnp.int32, (wide, L), 1)
            return tuple(
                old + jnp.sum(
                    jnp.where(slot == lanes + k * L, leak, 0.0).reshape(wide // 8, 8, L), axis=0
                )
                for k, old in enumerate(sums)
            )

        sums = lax.fori_loop(
            0, segs // wide, leaks, tuple(jnp.zeros((8, L), F32) for _ in range(3 * h))
        )
        own = jnp.concatenate(
            [jnp.sum(x, axis=0, keepdims=True) for x in sums] + [jnp.zeros((8 - 3 * h, L), F32)],
            axis=0,
        )
        su_send[step] = own
        su_copies = []
        for k, by in enumerate(SUM_STEPS):
            c = remote(
                su_send.at[step],
                su_recv.at[step, k],
                su_s.at[step, k],
                su_r.at[step, k],
                other(0, by),
            )
            c.start()
            su_copies.append(c)
        started += su_copies
        if step == 0:
            several(rows * tiles // L, 3, build_put)
            locals_[1].wait()
            locals_[2].wait()
            several(tiles, 2, start_grid)
            waiting = send_halo(0, (ga, inv))
            started += waiting
        else:
            for c in waiting:
                c.wait_recv()
            take_halo(2, (ga,))
        clear_halo(rhs)
        for c in su_copies:
            c.wait_recv()
        pad = jnp.zeros((8 - 3 * h, L), F32)
        from_l, from_r, from_ll, from_rr = (su_recv.at[step, k] for k in range(4))
        total = own + jnp.concatenate(
            [
                from_l[h : 2 * h] + from_ll[2 * h : 3 * h],
                from_l[2 * h : 3 * h] + from_r[0:h],
                from_r[h : 2 * h] + from_rr[0:h],
                pad,
            ],
            axis=0,
        )
        x = flow_w - total
        soft = jnp.maximum(x, 0.0) + jnp.log1p(jnp.exp(-jnp.abs(x)))
        sec_w = bed_w + jnp.sqrt(1.0 + soft) - 1.0
        spread(sec_w, True)

        def sources(t, _):
            c = pl.ds(pl.multiple_of(t * L, L), L)
            rhs[inner, c] = supply[inner, c] + scattered(t)
            return 0

        several(tiles, 2, sources)
        mine = send_halo(1 + 2 * step, (rhs,))
        started += mine
        if step == 0:
            for c in waiting:
                c.wait_recv()
            take_halo(0, (ga, inv))
        bufs = (ga, gb)
        for k in range(SWEEPS):
            last = step == PICARD - 1 and k == SWEEPS - 1
            sweep(bufs[k % 2], bufs[(k + 1) % 2], last)
            if k == 0:
                for c in mine:
                    c.wait_recv()
                take_halo(1 + 2 * step, (rhs,))
                for r, c in (
                    (slice(0, E), slice(0, cols + L)),
                    (slice(E + rows, 2 * E + rows), slice(0, cols + L)),
                    (inner, slice(cols, cols + L)),
                ):
                    gb[r, c] = gb[r, c] + rhs[r, c] * inv[r, c]
        if step < PICARD - 1:
            waiting = send_halo(2, (ga,))
            started += waiting
            several(tiles, 4, fill_heads)

    out_sec[...] = sec_w[h : 2 * h, :]
    for c in started:
        c.wait_send()


def leave(head, sec, out_head, out_sec, sems):
    part = head.shape[0] // PARTS
    copies = [pltpu.make_async_copy(sec, out_sec, sems.at[PARTS])]
    for k in range(PARTS):
        r = slice(k * part, (k + 1) * part)
        copies.append(pltpu.make_async_copy(head.at[r, :], out_head.at[r, :], sems.at[k]))
    for c in copies:
        c.start()
    for c in copies:
        c.wait()


def body(n_row, n_col, head, rech, stor, blk, mask, cond, reach, bed, sec, net, inflow):
    rows, cols = head.shape
    segs = blk.shape[0]
    reaches = bed.shape[0]
    blocks = rows * cols // L
    h = reaches // L
    vmem = pl.BlockSpec(memory_space=pltpu.VMEM)
    grid = pltpu.VMEM((rows + 2 * E, cols + L), F32)
    scratch = [
        pltpu.VMEM((segs // L, L), F32),
        pltpu.VMEM((segs, blocks), BF16),
        pltpu.VMEM((blocks, segs), BF16),
        pltpu.VMEM((segs, L), F32),
        pltpu.VMEM((segs, L), jnp.int32),
        pltpu.VMEM((segs, L), F32),
        pltpu.VMEM((blocks, 2 * L), BF16),
        pltpu.VMEM((segs, 2 * L), BF16),
        grid,
        grid,
        grid,
        grid,
        grid,
        pltpu.VMEM((3, 8, L), F32),
        pltpu.VMEM((2, 3, 8, L), F32),
        pltpu.VMEM((PICARD, 8, L), F32),
        pltpu.VMEM((PICARD, 4, 8, L), F32),
    ]
    for n in COUNTS:
        for _ in range(2):
            scratch += [
                pltpu.VMEM((2, n, E, cols), F32),
                pltpu.VMEM((2, n, E, rows), F32),
                pltpu.VMEM((4, n, E, L), F32),
            ]
    dma = pltpu.SemaphoreType.DMA
    scratch += [
        dma((2,)),
        dma((2,)),
        dma((PICARD, 4)),
        dma((PICARD, 4)),
        dma((len(COUNTS), 8)),
        dma((len(COUNTS), 8)),
        dma((3,)),
    ]
    out_head, out_sec = pl.pallas_call(
        functools.partial(kernel, n_row, n_col, inflow.shape[0]),
        out_shape=(
            jax.ShapeDtypeStruct((rows, cols), F32),
            jax.ShapeDtypeStruct((h, L), F32),
        ),
        in_specs=[pl.BlockSpec(memory_space=pl.ANY)] * 3 + [vmem] * 7 + [pl.BlockSpec(memory_space=pltpu.SMEM)],
        out_specs=(vmem, vmem),
        scratch_shapes=scratch,
        compiler_params=pltpu.CompilerParams(
            collective_id=0, has_side_effects=True, vmem_limit_bytes=56 * 1024 * 1024
        ),
    )(
        head,
        rech,
        stor,
        blk.reshape(segs // L, L),
        mask,
        cond,
        reach.reshape(segs // L, L),
        bed.reshape(h, L),
        sec.reshape(h, L),
        net.reshape(h, L),
        inflow,
    )
    anywhere = pl.BlockSpec(memory_space=pl.ANY)
    out_head, out_sec = pl.pallas_call(
        leave,
        out_shape=(
            jax.ShapeDtypeStruct((rows, cols), F32),
            jax.ShapeDtypeStruct((h, L), F32),
        ),
        in_specs=[anywhere] * 2,
        out_specs=(anywhere,) * 2,
        scratch_shapes=[pltpu.SemaphoreType.DMA((PARTS + 1,))],
        compiler_params=pltpu.CompilerParams(vmem_limit_bytes=60 * 1024 * 1024),
    )(out_head, out_sec)
    return out_head, out_sec.reshape(reaches)


def solution(mesh):
    placed = (
        P("row", "col"),
        P("row", "col"),
        P("row", "col"),
        P(("row", "col")),
        P(("row", "col"), None),
        P(("row", "col"), None),
        P(("row", "col")),
        P(("row", "col")),
        P(("row", "col")),
        P(("row", "col")),
        P(),
    )
    return jax.shard_map(
        functools.partial(body, mesh.shape["row"], mesh.shape["col"]),
        mesh=mesh,
        in_specs=placed,
        out_specs=(P("row", "col"), P(("row", "col"))),
        check_vma=False,
    )
```

```python
import functools

import jax
import jax.numpy as jnp
from jax import lax
from jax.experimental import pallas as pl
from jax.experimental.pallas import tpu as pltpu
from jax.sharding import PartitionSpec as P

PICARD = 2
SWEEPS = 4
L = 128
E = 8
F32 = jnp.float32
BF16 = jnp.bfloat16

DIRS = ((-1, 0), (1, 0), (0, -1), (0, 1), (-1, -1), (-1, 1), (1, -1), (1, 1))
COUNTS = (2, 1, 1, 1)
PARTS = 8
SUM_STEPS = (1, -1, 2, -2)


def several(count, most, one):
    unit = max(u for u in range(1, most + 1) if count % u == 0)

    def some(g, _):
        for u in range(unit):
            one(g * unit + u, 0)
        return 0

    lax.fori_loop(0, count // unit, some, 0)


def split(x):
    hi = x.astype(BF16)
    return hi, (x - hi.astype(F32)).astype(BF16)


def kernel(
    n_row,
    n_col,
    nets,
    head_in,
    rech,
    stor,
    blk,
    mask,
    conduct,
    reach,
    bed,
    sec0,
    net,
    inflow,
    out_head,
    out_sec,
    place,
    pick,
    put,
    weight,
    slots,
    secseg,
    heads2,
    vals2,
    ga,
    gb,
    supply,
    rhs,
    inv,
    st_send,
    st_recv,
    su_send,
    su_recv,
    *rest,
):
    halo = [rest[6 * e : 6 * e + 6] for e in range(len(COUNTS))]
    st_s, st_r, su_s, su_r, ha_s, ha_r, lo_s = rest[6 * len(COUNTS) :]
    rows, cols = head_in.shape
    tiles = cols // L
    shift = tiles.bit_length() - 1
    segs = mask.shape[0]
    chunks = segs // L
    h = bed.shape[0]
    reaches = h * L
    ri = lax.axis_index("row")
    ci = lax.axis_index("col")

    def other(dr, dc):
        return (lax.rem(ri + (dr + n_row), n_row), lax.rem(ci + (dc + n_col), n_col))

    partners = list(DIRS) + [(0, 2), (0, -2)]
    barrier = pltpu.get_barrier_semaphore()
    for dr, dc in partners:
        pl.semaphore_signal(
            barrier, inc=1, device_id=other(dr, dc), device_id_type=pl.DeviceIdType.MESH
        )

    def remote(src, dst, send, recv, to):
        return pltpu.make_async_remote_copy(
            src_ref=src,
            dst_ref=dst,
            send_sem=send,
            recv_sem=recv,
            device_id=to,
            device_id_type=pl.DeviceIdType.MESH,
        )

    started = []
    inner = slice(E, E + rows)
    locals_ = [
        pltpu.make_async_copy(x, y.at[inner, 0:cols], lo_s.at[k])
        for k, (x, y) in enumerate(((head_in, ga), (stor, inv), (rech, supply)))
    ]
    for c in locals_:
        c.start()

    lane = lax.broadcasted_iota(jnp.int32, (L, L), 1)
    sub = lax.broadcasted_iota(jnp.int32, (L, L), 0)
    sub8 = lax.broadcasted_iota(jnp.int32, (8, L), 0)

    net_own = net[...]
    flow = jnp.zeros(net_own.shape, F32)
    for n in range(nets):
        flow = jnp.where(net_own == n, inflow[n], flow)
    st_send[...] = jnp.zeros_like(st_send)
    st_send[0, 0:h] = bed[...]
    st_send[1, 0:h] = flow
    st_send[2, 0:h] = sec0[...]

    b = blk[...]
    place[...] = ((b & (tiles - 1)) * rows + (b >> shift)).astype(F32)

    pl.semaphore_wait(barrier, len(partners))
    st_copies = []
    for k, step in enumerate((1, -1)):
        c = remote(st_send, st_recv.at[k], st_s.at[k], st_r.at[k], other(0, step))
        c.start()
        st_copies.append(c)
    started += st_copies

    own_base = (ri * n_col + ci) * reaches

    def prep(j, _):
        r = pl.ds(pl.multiple_of(j * L, L), L)
        w = mask[r, :].astype(F32) * conduct[r, :]
        weight[r, :] = w
        hi, lo = split(w)
        vals2[r, 0:L] = hi
        vals2[r, L : 2 * L] = lo
        u = reach[pl.ds(j, 1), :] - own_base + reaches
        u = jnp.where(u < 0, u + n_col * reaches, u)
        u = jnp.where(u >= n_col * reaches, u - n_col * reaches, u)
        slots[r, :] = jnp.broadcast_to(u.astype(F32), (L, L)).T.astype(jnp.int32)
        return 0

    several(chunks, 4, prep)

    def build_put(q, _):
        base = q * L
        r = pl.ds(pl.multiple_of(base, L), L)
        for j in range(chunks):
            p = place[j : j + 1, :].astype(jnp.int32) - base
            put[r, j * L : (j + 1) * L] = jnp.where(sub == p, 1.0, 0.0).astype(BF16)
        return 0


    def scattered(t):
        r = pl.ds(pl.multiple_of(t * rows, L), rows)
        both = jnp.dot(put[r, :], vals2[...], preferred_element_type=F32)
        return both[:, 0:L] + both[:, L : 2 * L]

    def start_grid(t, _):
        c = pl.ds(pl.multiple_of(t * L, L), L)
        cond = scattered(t)
        s = inv[inner, c]
        supply[inner, c] = s * ga[inner, c] + supply[inner, c]
        inv[inner, c] = 1.0 / (4.0 + s + cond)
        return 0

    def send_halo(e, arrays):
        s_row, s_col, s_dia, r_row, r_col, r_dia = halo[e]
        for a, x in enumerate(arrays):
            top = x[E : 2 * E, 0:cols]
            bot = x[rows : rows + E, 0:cols]
            s_row[0, a] = top
            s_row[1, a] = bot
            s_col[0, a] = x[inner, 0:L].T[0:E, :]
            s_col[1, a] = x[inner, cols - L : cols].T[L - E : L, :]
            s_dia[0, a] = top[:, 0:L]
            s_dia[1, a] = top[:, cols - L : cols]
            s_dia[2, a] = bot[:, 0:L]
            s_dia[3, a] = bot[:, cols - L : cols]
        copies = []
        for d, (dr, dc) in enumerate(DIRS):
            if dc == 0:
                src, dst = s_row.at[d], r_row.at[d]
            elif dr == 0:
                src, dst = s_col.at[d - 2], r_col.at[d - 2]
            else:
                src, dst = s_dia.at[d - 4], r_dia.at[d - 4]
            c = remote(src, dst, ha_s.at[e, d], ha_r.at[e, d], other(dr, dc))
            c.start()
            copies.append(c)
        return copies

    above = ri > 0
    below = ri < n_row - 1
    lefts = ci > 0
    rights = ci < n_col - 1

    def keep(flag, x):
        return x * jnp.where(flag, 1.0, 0.0).astype(F32)

    def take_halo(e, arrays):
        _, _, _, r_row, r_col, r_dia = halo[e]
        lane8 = lax.broadcasted_iota(jnp.int32, (E, L), 1)
        for a, x in enumerate(arrays):
            x[E + rows : 2 * E + rows, 0:cols] = keep(below, r_row[0, a])
            x[0:E, 0:cols] = keep(above, r_row[1, a])
            beside = jnp.concatenate(
                [
                    keep(rights, r_col[0, a]),
                    jnp.zeros((L - 2 * E, rows), F32),
                    keep(lefts, r_col[1, a]),
                ],
                axis=0,
            )
            x[inner, cols : cols + L] = beside.T
            low = jnp.where(lane8 < L // 2, keep(rights, r_dia[0, a]), keep(lefts, r_dia[1, a]))
            high = jnp.where(lane8 < L // 2, keep(rights, r_dia[2, a]), keep(lefts, r_dia[3, a]))
            x[E + rows : 2 * E + rows, cols : cols + L] = keep(below, low)
            x[0:E, cols : cols + L] = keep(above, high)

    def build_pick(j, _):
        r = pl.ds(pl.multiple_of(j * L, L), L)
        p = jnp.broadcast_to(place[pl.ds(j, 1), :], (L, L)).T.astype(jnp.int32)
        for q in range(rows * tiles // L):
            pick[r, q * L : (q + 1) * L] = jnp.where(p == lane + q * L, 1.0, 0.0).astype(BF16)
        return 0

    several(chunks, 2, build_pick)

    def fill_heads(t, _):
        c = pl.ds(pl.multiple_of(t * L, L), L)
        r = pl.ds(pl.multiple_of(t * rows, L), rows)
        hi, lo = split(ga[inner, c])
        heads2[r, 0:L] = hi
        heads2[r, L : 2 * L] = lo
        return 0

    locals_[0].wait()
    several(tiles, 4, fill_heads)

    for c in st_copies:
        c.wait_recv()

    def window(k):
        pad = jnp.zeros((8 - 3 * h, L), F32)
        return jnp.concatenate(
            [st_recv[0, k, 0:h], st_send[k, 0:h], st_recv[1, k, 0:h], pad], axis=0
        )

    bed_w = window(0)
    flow_w = window(1)
    sec_w = window(2)

    def spread(sec, fill):
        def one(j, _):
            r = pl.ds(pl.multiple_of(j * L, L), L)
            slot = slots[r, :]
            got = jnp.zeros((L, L), F32)
            for k in range(3 * h):
                got = jnp.where(slot == lane + k * L, sec[k : k + 1, :], got)
            per = jnp.broadcast_to(jnp.sum(got, axis=1, keepdims=True), (L, L))
            secseg[r, :] = per
            if fill:
                hi, lo = split(weight[r, :] * per)
                vals2[r, 0:L] = hi
                vals2[r, L : 2 * L] = lo
            return 0

        several(chunks, 8, one)

    spread(sec_w, False)

    wide = 4 * L if segs % (4 * L) == 0 else L
    groups = (2 * E + rows) // 8

    def sweep(src, dst, last):
        first = 1 if last else 0
        count = groups - 2 * first
        unit = max(u for u in range(1, 13) if count % u == 0)

        def some(g, carry):
            prev, cur = carry
            for u in range(unit):
                i = first + g * unit + u
                r = pl.ds(pl.multiple_of(i * 8, 8), 8)
                nxt = src[pl.ds(pl.multiple_of(jnp.minimum(i + 1, groups - 1) * 8, 8), 8), :]
                s = lax.broadcasted_iota(jnp.int32, cur.shape, 0)
                up = pltpu.roll(jnp.where(s == 7, prev, cur), 1, 0)
                down = pltpu.roll(jnp.where(s == 0, nxt, cur), 7, 0)
                left = pltpu.roll(cur, 1, 1)
                right = pltpu.roll(cur, cols + L - 1, 1)
                new = (((up + down) + (left + right)) + rhs[r, :]) * inv[r, :]
                if last:
                    out_head[pl.ds(pl.multiple_of(i * 8 - E, 8), 8), :] = new[:, 0:cols]
                else:
                    dst[r, :] = new
                prev, cur = cur, nxt
            return prev, cur

        lax.fori_loop(0, count // unit, some, (src[0:8, :], src[8 * first : 8 * first + 8, :]))

    def clear_halo(x):
        x[0:E, :] = jnp.zeros((E, cols + L), F32)
        x[E + rows : 2 * E + rows, :] = jnp.zeros((E, cols + L), F32)
        x[inner, cols : cols + L] = jnp.zeros((rows, L), F32)

    for step in range(PICARD):

        def leaks(j, sums):
            r = pl.ds(pl.multiple_of(j * wide, L), wide)
            both = jnp.dot(pick[r, :], heads2[...], preferred_element_type=F32)
            got = both[:, 0:L] + both[:, L : 2 * L]
            leak = jnp.sum(weight[r, :] * (secseg[r, :] - got), axis=1, keepdims=True)
            slot = slots[r, :]
            lanes = lax.broadcasted_iota(jnp.int32, (wide, L), 1)
            return tuple(
                old + jnp.sum(
                    jnp.where(slot == lanes + k * L, leak, 0.0).reshape(wide // 8, 8, L), axis=0
                )
                for k, old in enumerate(sums)
            )

        sums = lax.fori_loop(
            0, segs // wide, leaks, tuple(jnp.zeros((8, L), F32) for _ in range(3 * h))
        )
        own = jnp.concatenate(
            [jnp.sum(x, axis=0, keepdims=True) for x in sums] + [jnp.zeros((8 - 3 * h, L), F32)],
            axis=0,
        )
        su_send[step] = own
        su_copies = []
        for k, by in enumerate(SUM_STEPS):
            c = remote(
                su_send.at[step],
                su_recv.at[step, k],
                su_s.at[step, k],
                su_r.at[step, k],
                other(0, by),
            )
            c.start()
            su_copies.append(c)
        started += su_copies
        if step == 0:
            several(rows * tiles // L, 3, build_put)
            locals_[1].wait()
            locals_[2].wait()
            several(tiles, 2, start_grid)
            waiting = send_halo(0, (ga, inv))
            started += waiting
        else:
            for c in waiting:
                c.wait_recv()
            take_halo(2, (ga,))
        clear_halo(rhs)
        for c in su_copies:
            c.wait_recv()
        pad = jnp.zeros((8 - 3 * h, L), F32)
        from_l, from_r, from_ll, from_rr = (su_recv.at[step, k] for k in range(4))
        total = own + jnp.concatenate(
            [
                from_l[h : 2 * h] + from_ll[2 * h : 3 * h],
                from_l[2 * h : 3 * h] + from_r[0:h],
                from_r[h : 2 * h] + from_rr[0:h],
                pad,
            ],
            axis=0,
        )
        x = flow_w - total
        soft = jnp.maximum(x, 0.0) + jnp.log1p(jnp.exp(-jnp.abs(x)))
        sec_w = bed_w + jnp.sqrt(1.0 + soft) - 1.0
        spread(sec_w, True)

        def sources(t, _):
            c = pl.ds(pl.multiple_of(t * L, L), L)
            rhs[inner, c] = supply[inner, c] + scattered(t)
            return 0

        several(tiles, 2, sources)
        mine = send_halo(1 + 2 * step, (rhs,))
        started += mine
        if step == 0:
            for c in waiting:
                c.wait_recv()
            take_halo(0, (ga, inv))
        bufs = (ga, gb)
        for k in range(SWEEPS):
            last = step == PICARD - 1 and k == SWEEPS - 1
            sweep(bufs[k % 2], bufs[(k + 1) % 2], last)
            if k == 0:
                for c in mine:
                    c.wait_recv()
                take_halo(1 + 2 * step, (rhs,))
                for r, c in (
                    (slice(0, E), slice(0, cols + L)),
                    (slice(E + rows, 2 * E + rows), slice(0, cols + L)),
                    (inner, slice(cols, cols + L)),
                ):
                    gb[r, c] = gb[r, c] + rhs[r, c] * inv[r, c]
        if step < PICARD - 1:
            waiting = send_halo(2, (ga,))
            started += waiting
            several(tiles, 4, fill_heads)

    out_sec[...] = sec_w[h : 2 * h, :]
    for c in started:
        c.wait_send()


def leave(head, sec, out_head, out_sec, held, held_sec, in_sems, out_sems):
    part = head.shape[0] // PARTS
    spans = [(sec, held_sec, out_sec)]
    for k in range(PARTS):
        r = slice(k * part, (k + 1) * part)
        spans.append((head.at[r, :], held.at[r, :], out_head.at[r, :]))
    ins = [pltpu.make_async_copy(x, y, in_sems.at[k]) for k, (x, y, _) in enumerate(spans)]
    outs = [pltpu.make_async_copy(y, z, out_sems.at[k]) for k, (_, y, z) in enumerate(spans)]
    for c in ins:
        c.start()
    for c, d in zip(ins, outs):
        c.wait()
        d.start()
    for d in outs:
        d.wait()


def body(n_row, n_col, head, rech, stor, blk, mask, cond, reach, bed, sec, net, inflow):
    rows, cols = head.shape
    segs = blk.shape[0]
    reaches = bed.shape[0]
    blocks = rows * cols // L
    h = reaches // L
    vmem = pl.BlockSpec(memory_space=pltpu.VMEM)
    grid = pltpu.VMEM((rows + 2 * E, cols + L), F32)
    scratch = [
        pltpu.VMEM((segs // L, L), F32),
        pltpu.VMEM((segs, blocks), BF16),
        pltpu.VMEM((blocks, segs), BF16),
        pltpu.VMEM((segs, L), F32),
        pltpu.VMEM((segs, L), jnp.int32),
        pltpu.VMEM((segs, L), F32),
        pltpu.VMEM((blocks, 2 * L), BF16),
        pltpu.VMEM((segs, 2 * L), BF16),
        grid,
        grid,
        grid,
        grid,
        grid,
        pltpu.VMEM((3, 8, L), F32),
        pltpu.VMEM((2, 3, 8, L), F32),
        pltpu.VMEM((PICARD, 8, L), F32),
        pltpu.VMEM((PICARD, 4, 8, L), F32),
    ]
    for n in COUNTS:
        for _ in range(2):
            scratch += [
                pltpu.VMEM((2, n, E, cols), F32),
                pltpu.VMEM((2, n, E, rows), F32),
                pltpu.VMEM((4, n, E, L), F32),
            ]
    dma = pltpu.SemaphoreType.DMA
    scratch += [
        dma((2,)),
        dma((2,)),
        dma((PICARD, 4)),
        dma((PICARD, 4)),
        dma((len(COUNTS), 8)),
        dma((len(COUNTS), 8)),
        dma((3,)),
    ]
    out_head, out_sec = pl.pallas_call(
        functools.partial(kernel, n_row, n_col, inflow.shape[0]),
        out_shape=(
            jax.ShapeDtypeStruct((rows, cols), F32),
            jax.ShapeDtypeStruct((h, L), F32),
        ),
        in_specs=[pl.BlockSpec(memory_space=pl.ANY)] * 3 + [vmem] * 7 + [pl.BlockSpec(memory_space=pltpu.SMEM)],
        out_specs=(vmem, vmem),
        scratch_shapes=scratch,
        compiler_params=pltpu.CompilerParams(
            collective_id=0, has_side_effects=True, vmem_limit_bytes=56 * 1024 * 1024
        ),
    )(
        head,
        rech,
        stor,
        blk.reshape(segs // L, L),
        mask,
        cond,
        reach.reshape(segs // L, L),
        bed.reshape(h, L),
        sec.reshape(h, L),
        net.reshape(h, L),
        inflow,
    )
    anywhere = pl.BlockSpec(memory_space=pl.ANY)
    out_head, out_sec = pl.pallas_call(
        leave,
        out_shape=(
            jax.ShapeDtypeStruct((rows, cols), F32),
            jax.ShapeDtypeStruct((h, L), F32),
        ),
        in_specs=[anywhere] * 2,
        out_specs=(anywhere,) * 2,
        scratch_shapes=[
            pltpu.VMEM((rows, cols), F32),
            pltpu.VMEM((h, L), F32),
            dma((PARTS + 1,)),
            dma((PARTS + 1,)),
        ],
        compiler_params=pltpu.CompilerParams(vmem_limit_bytes=60 * 1024 * 1024),
    )(out_head, out_sec)
    return out_head, out_sec.reshape(reaches)


def solution(mesh):
    placed = (
        P("row", "col"),
        P("row", "col"),
        P("row", "col"),
        P(("row", "col")),
        P(("row", "col"), None),
        P(("row", "col"), None),
        P(("row", "col")),
        P(("row", "col")),
        P(("row", "col")),
        P(("row", "col")),
        P(),
    )
    return jax.shard_map(
        functools.partial(body, mesh.shape["row"], mesh.shape["col"]),
        mesh=mesh,
        in_specs=placed,
        out_specs=(P("row", "col"), P(("row", "col"))),
        check_vma=False,
    )
```
